256 devices in a mesh: req: 16 (over y, x), lend: 16 (over z, core).
Axes of the slice: x: 4, y: 4, z: 8, core: 2. Of those that a mesh axis runs over, the one named last changes fastest.
Arguments:
- queries: bfloat16 [4, 256, 4096], P(None, ('req', 'lend')), may hold values from -150 to 150
- new_keys: bfloat16 [4, 256, 512], P(None, ('req', 'lend')), may hold values from -6 to 6
- new_values: bfloat16 [4, 256, 512], P(None, ('req', 'lend')), may hold values from -6 to 6
- key_pool: bfloat16 [12288, 128, 512], P(('req', 'lend')), may hold values from -6 to 6
- value_pool: bfloat16 [12288, 128, 512], P(('req', 'lend')), may hold values from -6 to 6
- key_scale: float32 [12288, 16, 128], P(('req', 'lend')), may hold values from 0.25 to 4
- value_scale: float32 [12288, 16, 128], P(('req', 'lend')), may hold values from 0.25 to 4
- page_request: int32 [12288], P(('req', 'lend')), may hold values from 0 to 255, as said below
- page_fill: int32 [12288], P(('req', 'lend')), may hold values from 0 to 128, as said below
- sinks: float32 [64], replicated, may hold values from 3 to 9
Outputs:
- attended: bfloat16 [4, 256, 4096], P(None, ('req', 'lend'))
The draws below stay inside these ranges and needn't reach their ends.
Inputs may be any that keep to these rules, and one draw needn't show every extreme that they name: `page_request`: A page slot on the device at flat index d = r * 16 + l (r its req index, l its lend index) holds tokens of a request owned by a device with req index r or with lend index l; request i is owned by flat device i. Some requests own far more pages than others. `page_fill`: free slots have 0. On each device the slots in use come first; every device uses three quarters or more of its 48 slots, and some device uses all of them.
All inputs are finite; a program needn't handle non-finite values.
Results may differ from the reference program's by a relative error of at most 0.0055.
The reference program's roundings to bfloat16 on the way count: a program that leaves them out, or rounds other values in their place, can miss the bound.
Values may be sent and summed in bfloat16 or wider, within the bound.
A program may use at most 128 MiB of HBM per device.

```python
import math
import jax
import jax.numpy as jnp
from jax import lax

HEADS = 64
KV_HEADS = 8
DH = 64
SBLOCK = 32
PAGE = 128
STEPS = 4
R_DEV = 1
PAGES_DEV = 48
KVD = 512
REQS = 256
POOL = 12288
N_REQ = 16
N_LEND = 16


def draw_queries(key, part):
    key = jax.random.fold_in(key, 37)
    normal_key = jax.random.fold_in(key, 0)
    base = jax.random.truncated_normal(normal_key, -5.0, 5.0, (STEPS, REQS, HEADS * DH), jnp.float32)
    return base.astype(jnp.bfloat16)


def draw_page_request(key, part):
    key = jax.random.fold_in(key, 11)
    class_key, pick_key = jax.random.split(key)
    classes = jax.random.randint(class_key, (REQS,), 0, 4)
    device = jnp.arange(POOL) // PAGES_DEV
    device_req = device // N_LEND
    device_lend = device % N_LEND
    row_count = N_LEND * R_DEV
    candidates = row_count + N_REQ * R_DEV
    picks = jax.random.randint(pick_key, (3, POOL), 0, candidates)
    column_pick = picks - row_count
    row_global = (device_req[None, :] * N_LEND + picks // R_DEV) * R_DEV + picks % R_DEV
    column_global = (column_pick // R_DEV * N_LEND + device_lend[None, :]) * R_DEV + column_pick % R_DEV
    chosen = jnp.where(picks < row_count, row_global, column_global)
    ranks = classes[chosen]
    winner = chosen[0]
    winner_rank = ranks[0]
    for index in range(1, 3):
        better = ranks[index] > winner_rank
        winner = jnp.where(better, chosen[index], winner)
        winner_rank = jnp.maximum(winner_rank, ranks[index])
    return winner.astype(jnp.int32)


def draw_page_fill(key, part):
    key = jax.random.fold_in(key, 23)
    used_key, full_key, partial_key, amount_key = jax.random.split(key, 4)
    device_count = N_REQ * N_LEND
    lowest = max(1, 3 * PAGES_DEV // 4)
    highest = PAGES_DEV + 1
    used = jax.random.randint(used_key, (device_count,), lowest, highest)
    full_device = jax.random.randint(full_key, (), 0, device_count)
    used = jnp.where(jnp.arange(device_count) == full_device, PAGES_DEV, used)
    local = jnp.arange(POOL) % PAGES_DEV
    device = jnp.arange(POOL) // PAGES_DEV
    live = local < used[device]
    partial_page = jax.random.randint(partial_key, (POOL,), 0, 4) == 0
    amount = jax.random.randint(amount_key, (POOL,), 1, PAGE + 1)
    fill = jnp.where(live, jnp.where(partial_page, amount, PAGE), 0)
    return fill.astype(jnp.int32)


def block_levels(key, extent, shards, low, top_value):
    gain = 1.0
    for axis_at, parts in shards:
        draws = jax.random.uniform(jax.random.fold_in(jax.random.fold_in(key, 6), axis_at), (parts,), jnp.float32, low / len(shards), top_value / len(shards))
        gain = gain * jnp.repeat(jnp.exp(draws), extent[axis_at] // parts).reshape((-1,) + (1,) * (len(extent) - 1 - axis_at))
    return gain


def noise(key, shape, scale, bound, pieces=(), held_as=jnp.bfloat16):
    drawn = scale * jax.random.normal(key, shape, jnp.float32)
    if pieces:
        drawn = drawn * block_levels(key, shape, pieces, -0.22, 0.18)
    return jnp.clip(drawn, -bound, bound).astype(held_as)


def setup_inputs(seed: int = 0) -> dict:
    key_of = jax.random.split(jax.random.key(seed), 11)
    return {
        "queries": draw_queries(jax.random.fold_in(key_of[10], 71), 0),
        "new_keys": noise(key_of[1], (STEPS, REQS, KVD), 1.0, 6.0, ((1, 256),)),
        "new_values": noise(key_of[2], (STEPS, REQS, KVD), 1.0, 6.0, ((1, 256),)),
        "key_pool": noise(key_of[3], (POOL, PAGE, KVD), 1.0, 6.0, ((0, 256),)),
        "value_pool": noise(key_of[4], (POOL, PAGE, KVD), 1.0, 6.0, ((0, 256),)),
        "key_scale": jnp.clip(jnp.exp(math.log(4.0) - 2.7725887 * jax.random.uniform(key_of[5], (POOL, KVD // SBLOCK, PAGE), jnp.float32) ** block_levels(key_of[5], (POOL, KVD // SBLOCK, PAGE), ((0, 256),), -0.2, 0.2)), 0.25, 4.0),
        "value_scale": jnp.clip(jnp.exp(math.log(4.0) - 2.7725887 * jax.random.uniform(key_of[6], (POOL, KVD // SBLOCK, PAGE), jnp.float32) ** block_levels(key_of[6], (POOL, KVD // SBLOCK, PAGE), ((0, 256),), -0.2, 0.2)), 0.25, 4.0),
        "page_request": draw_page_request(jax.random.fold_in(key_of[10], 71), 0),
        "page_fill": draw_page_fill(jax.random.fold_in(key_of[10], 71), 0),
        "sinks": jnp.clip(jax.random.uniform(key_of[9], (HEADS,), jnp.float32, 3.0, 9.0), 3.0, 9.0),
    }


FLOOR = -1.0e30
SCORE_SCALE = 0.125


def dequantize(pool, scales):
    pages, tokens, width = pool.shape
    blocks = scales.shape[1]
    spread = jnp.swapaxes(scales, 1, 2)[..., None]
    shaped = pool.astype(jnp.float32).reshape(pages, tokens, blocks, width // blocks)
    return (shaped * spread).reshape(pages, tokens, width).astype(jnp.bfloat16)


def page_terms(page_query, keys_deq, values_deq, fills):
    steps, pages, qwidth = page_query.shape
    tokens = keys_deq.shape[1]
    groups = KV_HEADS
    per_group = HEADS // KV_HEADS
    query_heads = page_query.astype(jnp.float32).reshape(steps, pages, groups, per_group, DH)
    key_heads = keys_deq.astype(jnp.float32).reshape(pages, tokens, groups, DH)
    value_heads = values_deq.astype(jnp.float32).reshape(pages, tokens, groups, DH)
    scores = jnp.einsum("spgae,ptge->spgat", query_heads, key_heads) * SCORE_SCALE
    valid = (jnp.arange(tokens)[None, :] < fills[:, None])[None, :, None, None, :]
    scores = jnp.where(valid, scores, FLOOR)
    top = jnp.max(scores, axis=-1)
    weights = jnp.where(valid, jnp.exp(scores - top[..., None]), 0.0)
    total = jnp.sum(weights, axis=-1)
    rounded = weights.astype(jnp.bfloat16).astype(jnp.float32)
    numer = jnp.einsum("spgat,ptge->spgae", rounded, value_heads)
    return (top.reshape(steps, pages, HEADS), total.reshape(steps, pages, HEADS),
            numer.reshape(steps, pages, HEADS, DH))


def gather_slots(top, total, numer, slot, count):
    page_top = jnp.moveaxis(top, 1, 0)
    page_total = jnp.moveaxis(total, 1, 0)
    page_numer = jnp.moveaxis(numer, 1, 0)
    best = jnp.maximum(jax.ops.segment_max(page_top, slot, num_segments=count), FLOOR)
    factor = jnp.exp(page_top - best[slot])
    summed = jax.ops.segment_sum(page_total * factor, slot, num_segments=count)
    weighted = jax.ops.segment_sum(page_numer * factor[..., None], slot, num_segments=count)
    return best, summed, weighted


def finalize(best, total, numer, queries, new_keys, new_values, sinks):
    steps, rows, qwidth = queries.shape
    groups = KV_HEADS
    per_group = HEADS // KV_HEADS
    query_heads = queries.astype(jnp.float32).reshape(steps, rows, groups, per_group, DH)
    fresh_keys = new_keys.astype(jnp.float32).reshape(steps, rows, groups, DH)
    fresh_values = new_values.astype(jnp.float32).reshape(steps, rows, groups, DH)
    fresh = jnp.einsum("srgae,urge->srgau", query_heads, fresh_keys) * SCORE_SCALE
    causal = (jnp.arange(steps)[None, :] <= jnp.arange(steps)[:, None])[:, None, None, None, :]
    fresh = jnp.where(causal, fresh, FLOOR)
    cached = jnp.transpose(best, (1, 0, 2)).reshape(steps, rows, groups, per_group)
    cached_total = jnp.transpose(total, (1, 0, 2)).reshape(steps, rows, groups, per_group)
    cached_numer = jnp.transpose(numer, (1, 0, 2, 3)).reshape(steps, rows, groups, per_group, DH)
    sink_logit = sinks.reshape(groups, per_group)
    highest = jnp.maximum(jnp.maximum(cached, jnp.max(fresh, axis=-1)), sink_logit)
    keep = jnp.exp(cached - highest)
    weights = jnp.where(causal, jnp.exp(fresh - highest[..., None]), 0.0)
    denom = cached_total * keep + jnp.sum(weights, axis=-1) + jnp.exp(sink_logit - highest)
    rounded = weights.astype(jnp.bfloat16).astype(jnp.float32)
    result = cached_numer * keep[..., None] + jnp.einsum("srgau,urge->srgae", rounded, fresh_values)
    return (result / denom[..., None]).reshape(steps, rows, qwidth).astype(jnp.bfloat16)


def reference(queries, new_keys, new_values, key_pool, value_pool, key_scale, value_scale,
              page_request, page_fill, sinks):
    device_count = N_REQ * N_LEND

    def visit(carry, index):
        start = (index * PAGES_DEV).astype(jnp.int32)
        keys = lax.dynamic_slice_in_dim(key_pool, start, PAGES_DEV, 0)
        values = lax.dynamic_slice_in_dim(value_pool, start, PAGES_DEV, 0)
        key_block_scale = lax.dynamic_slice_in_dim(key_scale, start, PAGES_DEV, 0)
        value_block_scale = lax.dynamic_slice_in_dim(value_scale, start, PAGES_DEV, 0)
        requests = lax.dynamic_slice_in_dim(page_request, start, PAGES_DEV, 0)
        fills = lax.dynamic_slice_in_dim(page_fill, start, PAGES_DEV, 0)
        page_query = jnp.take(queries, requests, axis=1)
        top, total, numer = page_terms(page_query, dequantize(keys, key_block_scale),
                                       dequantize(values, value_block_scale), fills)
        block_best, block_total, block_numer = gather_slots(top, total, numer, requests, REQS)
        best, summed, weighted = carry
        newest = jnp.maximum(best, block_best)
        old_factor = jnp.exp(best - newest)
        add_factor = jnp.exp(block_best - newest)
        summed = summed * old_factor + block_total * add_factor
        weighted = weighted * old_factor[..., None] + block_numer * add_factor[..., None]
        return (newest, summed, weighted), None

    start_carry = (jnp.full((REQS, STEPS, HEADS), FLOOR, jnp.float32),
                   jnp.zeros((REQS, STEPS, HEADS), jnp.float32),
                   jnp.zeros((REQS, STEPS, HEADS, DH), jnp.float32))
    final_carry, _ = lax.scan(visit, start_carry, jnp.arange(device_count).astype(jnp.int32))
    best, summed, weighted = final_carry
    return finalize(best, summed, weighted, queries, new_keys, new_values, sinks)
```

```python
import functools

import jax
import jax.numpy as jnp
from jax import lax
from jax.experimental import pallas as pl
from jax.experimental.pallas import tpu as pltpu
from jax.sharding import PartitionSpec as P

FLOOR = -1e30
SCORE_SCALE = 0.125
BF = jnp.bfloat16
F32 = jnp.float32
MESH = pl.DeviceIdType.MESH
GROUPS = 4
MSG = 80


def kernel(
    dims,
    ints,
    qt,
    fresh_kv,
    sinks,
    k_hbm,
    v_hbm,
    ks_hbm,
    vs_hbm,
    out,
    kraw,
    vraw,
    ks,
    vs,
    kd,
    vd,
    q0,
    q1,
    num0,
    num1,
    st0,
    st1,
    stage,
    landed,
    load_sem,
    qsend,
    qrecv,
    psend,
    precv,
):
    n_req, n_lend, pages, chunk, unroll, dunroll = dims
    chunks = pages // chunk
    slots = n_lend + n_req
    req = lax.axis_index("req")
    lend = lax.axis_index("lend")
    qbuf = (q0, q1)
    num = (num0, num1)
    st = (st0, st1)

    def loads(c):
        sl = pl.ds(c * chunk, chunk)
        pairs = ((k_hbm, kraw), (v_hbm, vraw), (ks_hbm, ks), (vs_hbm, vs))
        return [
            pltpu.make_async_copy(src.at[sl], dst.at[sl], load_sem.at[i, c])
            for i, (src, dst) in enumerate(pairs)
        ]

    for c in range(chunks):
        for copy in loads(c):
            copy.start()

    row_peer = lambda k: (req, lax.rem(lend + k, n_lend))
    col_peer = lambda k: (lax.rem(req + k, n_req), lend)

    barrier = pltpu.get_barrier_semaphore()

    def greet(peer):
        def go(k, carry):
            pl.semaphore_signal(barrier, inc=1, device_id=peer(k), device_id_type=MESH)
            return carry

        return go

    lax.fori_loop(1, n_lend, greet(row_peer), 0)
    lax.fori_loop(1, n_req, greet(col_peer), 0)
    for h in range(2):
        qbuf[h][lend] = qt[h]
        qbuf[h][n_lend + req] = qt[h]
    pl.semaphore_wait(barrier, n_lend + n_req - 2)

    def q_row(h, k):
        return pltpu.make_async_remote_copy(
            src_ref=qt.at[h],
            dst_ref=qbuf[h].at[lend],
            send_sem=qsend.at[h, k],
            recv_sem=qrecv.at[h, k],
            device_id=row_peer(k),
            device_id_type=MESH,
        )

    def q_col(h, k):
        return pltpu.make_async_remote_copy(
            src_ref=qt.at[h],
            dst_ref=qbuf[h].at[n_lend + req],
            send_sem=qsend.at[h, n_lend + k],
            recv_sem=qrecv.at[h, n_lend + k],
            device_id=col_peer(k),
            device_id_type=MESH,
        )

    def loop(lo, hi, fn):
        def go(k, carry):
            fn(k)
            return carry

        lax.fori_loop(lo, hi, go, 0)

    for h in range(2):
        loop(1, n_lend, lambda k: q_row(h, k).start())
        loop(1, n_req, lambda k: q_col(h, k).start())

    blk = lax.broadcasted_iota(jnp.int32, (48, 512), 0) % 16
    chan = lax.broadcasted_iota(jnp.int32, (48, 512), 1) // 32
    spread = (blk == chan).astype(F32).astype(BF)

    def dequant(p):
        s = ks[p]
        hi = s.astype(BF)
        rest = s - hi.astype(F32)
        mid = rest.astype(BF)
        low = (rest - mid.astype(F32)).astype(BF)
        parts = jnp.concatenate([hi, mid, low], axis=0)
        wide = lax.dot_general(
            parts, spread, (((0,), (0,)), ((), ())), preferred_element_type=F32
        )
        kd[p] = (kraw[p].astype(F32) * wide).astype(BF)
        vt = vraw[p].T
        sv = jnp.broadcast_to(vs[p][:, None, :], (16, 32, 128)).reshape(512, 128)
        vd[p] = (vt.astype(F32) * sv).astype(BF)

    for c in range(chunks):
        for copy in loads(c):
            copy.wait()

        def some(i, carry):
            for j in range(dunroll):
                dequant(c * chunk + i * dunroll + j)
            return carry

        lax.fori_loop(0, chunk // dunroll, some, 0)

    lane_group = lax.broadcasted_iota(jnp.int32, (64, 128), 1) // 32
    token = lax.broadcasted_iota(jnp.int32, (128, 128), 0)

    def block_diagonal(q):
        zero = jnp.zeros_like(q)
        return jnp.concatenate(
            [jnp.where(lane_group == g, q, zero) for g in range(GROUPS)], axis=0
        )

    def fold(wide):
        x = wide[0:64]
        for g in range(1, GROUPS):
            x = jnp.where(lane_group == g, wide[64 * g : 64 * g + 64], x)
        return x

    def page(p, h):
        slot = ints[0, p]
        fill = ints[2, p]
        qb = block_diagonal(qbuf[h][slot])
        s = jnp.dot(kd[p, :, h * 256 : h * 256 + 256], qb, preferred_element_type=F32)
        s = jnp.where(token < fill, s, FLOOR)
        top = jnp.max(s, axis=0, keepdims=True)
        w = jnp.exp(s - top)
        total = jnp.sum(w, axis=0, keepdims=True)
        wide = jnp.dot(
            vd[p, h * 256 : h * 256 + 256, :], w.astype(BF), preferred_element_type=F32
        )
        return top, total, fold(wide)

    def update(p, h, top, total, x):
        prev = ints[1, p]
        fill = ints[2, p]
        prev_stat = st[h][prev]
        prev_top, prev_total = prev_stat[0:1], prev_stat[1:2]
        best = jnp.maximum(prev_top, top)
        fa = jnp.exp(prev_top - best)
        fb = jnp.where(fill > 0, jnp.exp(top - best), 0.0)
        st[h][p, 0:1, :] = best
        st[h][p, 1:2, :] = prev_total * fa + total * fb
        num[h][p] = num[h][prev] * fa + x * fb

    row16 = lax.broadcasted_iota(jnp.int32, (16, 128), 0)

    def pack(best, total, x):
        bh = best.astype(BF).astype(F32)
        bm = (best - bh).astype(BF).astype(F32)
        bl = best - bh - bm
        th = total.astype(BF).astype(F32)
        tm = total - th
        rows = jnp.zeros((16, 128), F32)
        for i, part in enumerate((bh, bm, bl, th, tm)):
            rows = jnp.where(row16 == i, part, rows)
        return jnp.concatenate([x.astype(BF), rows.astype(BF)], axis=0)

    def unpack(msg):
        x = msg[0:64].astype(F32)
        rows = msg[64:80].astype(F32)
        best = rows[0:1] + rows[1:2] + rows[2:3]
        total = rows[3:4] + rows[4:5]
        return best, total, x

    def partial_copy(h, k, peer):
        return pltpu.make_async_remote_copy(
            src_ref=stage.at[h, k],
            dst_ref=landed.at[h, k],
            send_sem=psend.at[h, k],
            recv_sem=precv.at[h, k],
            device_id=peer,
            device_id_type=MESH,
        )

    def p_row(h, k):
        return partial_copy(h, k, row_peer(k))

    def p_col(h, k):
        return partial_copy(h, n_lend + k, col_peer(k))

    def fill_stage(h, k, slot):
        at = ints[3, slot]
        stat = st[h][at]
        stage[h, k] = pack(stat[0:1], stat[1:2], num[h][at])

    u16 = lax.broadcasted_iota(jnp.int32, (16, 128), 0)
    step16 = (lax.broadcasted_iota(jnp.int32, (16, 128), 1) // 8) % 4

    def fresh(h):
        qb = block_diagonal(qt[h])
        s = jnp.dot(
            fresh_kv[0, :, h * 256 : h * 256 + 256], qb, preferred_element_type=F32
        )
        s = jnp.where(u16 <= step16, s, FLOOR)
        top = jnp.max(s, axis=0, keepdims=True)
        w = jnp.exp(s - top)
        total = jnp.sum(w, axis=0, keepdims=True)
        wide = lax.dot_general(
            fresh_kv[1, :, h * 256 : h * 256 + 256],
            w.astype(BF),
            (((0,), (0,)), ((), ())),
            preferred_element_type=F32,
        )
        return top, total, fold(wide)

    for h in range(2):
        loop(1, n_lend, lambda k: q_row(h, k).wait_recv())
        loop(1, n_req, lambda k: q_col(h, k).wait_recv())
        num[h][pages] = jnp.zeros((64, 128), F32)
        st[h][pages] = jnp.where(
            lax.broadcasted_iota(jnp.int32, (8, 128), 0) == 0, FLOOR, 0.0
        )

        def some_pages(i, carry):
            done = [page(i * unroll + j, h) for j in range(unroll)]
            for j in range(unroll):
                update(i * unroll + j, h, *done[j])
            return carry

        lax.fori_loop(0, pages // unroll, some_pages, 0)

        def send_row(k):
            fill_stage(h, k, lax.rem(lend + k, n_lend))
            p_row(h, k).start()

        def send_col(k):
            fill_stage(h, n_lend + k, n_lend + lax.rem(req + k, n_req))
            p_col(h, k).start()

        loop(1, n_lend, send_row)
        loop(1, n_req, send_col)

    for h in range(2):
        at = ints[3, lend]
        own = st[h][at]
        sink = sinks[h, 0:1, :]
        ftop, ftotal, fx = fresh(h)
        top = jnp.maximum(jnp.maximum(own[0:1], ftop), sink)
        fa = jnp.exp(own[0:1] - top)
        fb = jnp.exp(ftop - top)
        total = own[1:2] * fa + ftotal * fb + jnp.exp(sink - top)
        x = num[h][at] * fa + fx * fb
        loop(1, n_lend, lambda k: p_row(h, k).wait_recv())
        loop(1, n_req, lambda k: p_col(h, k).wait_recv())

        def absorb(k, carry):
            top, total, x = carry
            ktop, ktotal, kx = unpack(landed[h, k])
            best = jnp.maximum(top, ktop)
            fa = jnp.exp(top - best)
            fb = jnp.exp(ktop - best)
            return best, total * fa + ktotal * fb, x * fa + kx * fb

        carry = lax.fori_loop(1, n_lend, absorb, (top, total, x))
        carry = lax.fori_loop(n_lend + 1, slots, absorb, carry)
        out[h] = (carry[2] / carry[1]).astype(BF)

    for h in range(2):
        loop(1, n_lend, lambda k: q_row(h, k).wait_send())
        loop(1, n_req, lambda k: q_col(h, k).wait_send())
        loop(1, n_lend, lambda k: p_row(h, k).wait_send())
        loop(1, n_req, lambda k: p_col(h, k).wait_send())


def on_device(
    queries,
    new_keys,
    new_values,
    key_pool,
    value_pool,
    key_scale,
    value_scale,
    page_request,
    page_fill,
    sinks,
):
    steps = queries.shape[0]
    pages = key_pool.shape[0]
    n_lend = lax.axis_size("lend")
    n_req = lax.axis_size("req")
    req_here = lax.axis_index("req")
    slots = n_lend + n_req
    owner_req = page_request // n_lend
    owner_lend = page_request % n_lend
    slot = jnp.where(owner_req == req_here, owner_lend, n_lend + owner_req)
    ids = jnp.arange(pages, dtype=jnp.int32)
    same = (slot[:, None] == slot[None, :]) & (ids[None, :] < ids[:, None])
    prev = jnp.max(jnp.where(same, ids[None, :], -1), axis=1)
    prev = jnp.where(prev < 0, pages, prev)
    hits = jnp.arange(pages, dtype=jnp.int32)[:, None] == slot[None, :]
    last = jnp.max(jnp.where(hits, ids[None, :], -1), axis=1)
    last = jnp.where(last < 0, pages, last)
    ints = jnp.stack([slot, prev, page_fill, last]).astype(jnp.int32)
    qt = queries.reshape(steps, 2, GROUPS, 8, 64)
    qt = jnp.transpose(qt, (1, 4, 2, 0, 3)).reshape(2, 64, 128)
    qt = qt * jnp.asarray(SCORE_SCALE, BF)
    fresh_kv = jnp.stack([new_keys[:, 0], new_values[:, 0]])
    fresh_kv = jnp.pad(fresh_kv, ((0, 0), (0, 12), (0, 0)))
    sink = jnp.broadcast_to(sinks.reshape(2, 1, GROUPS, 1, 8), (2, 8, GROUPS, steps, 8))
    sink = sink.reshape(2, 8, 128)

    chunk = 6 if pages % 6 == 0 else 4
    dims = (n_req, n_lend, pages, chunk, 12 if pages % 12 == 0 else 4, chunk)
    smem = pl.BlockSpec(memory_space=pltpu.SMEM)
    vmem = pl.BlockSpec(memory_space=pltpu.VMEM)
    hbm = pl.BlockSpec(memory_space=pl.ANY)
    dma = pltpu.SemaphoreType.DMA
    half = pl.pallas_call(
        functools.partial(kernel, dims),
        out_shape=jax.ShapeDtypeStruct((2, 64, 128), BF),
        in_specs=[smem, vmem, vmem, vmem, hbm, hbm, hbm, hbm],
        out_specs=vmem,
        scratch_shapes=[
            pltpu.VMEM((pages, 128, 512), BF),
            pltpu.VMEM((pages, 128, 512), BF),
            pltpu.VMEM((pages, 16, 128), F32),
            pltpu.VMEM((pages, 16, 128), F32),
            pltpu.VMEM((pages, 128, 512), BF),
            pltpu.VMEM((pages, 512, 128), BF),
            pltpu.VMEM((slots, 64, 128), BF),
            pltpu.VMEM((slots, 64, 128), BF),
            pltpu.VMEM((pages + 1, 64, 128), F32),
            pltpu.VMEM((pages + 1, 64, 128), F32),
            pltpu.VMEM((pages + 1, 8, 128), F32),
            pltpu.VMEM((pages + 1, 8, 128), F32),
            pltpu.VMEM((2, slots, MSG, 128), BF),
            pltpu.VMEM((2, slots, MSG, 128), BF),
            dma((4, pages // chunk)),
            dma((2, slots)),
            dma((2, slots)),
            dma((2, slots)),
            dma((2, slots)),
        ],
        compiler_params=pltpu.CompilerParams(
            collective_id=0, has_side_effects=True, vmem_limit_bytes=50 * 2**20
        ),
    )(ints, qt, fresh_kv, sink, key_pool, value_pool, key_scale, value_scale)
    out = half.reshape(2, 64, GROUPS, steps, 8)
    return jnp.transpose(out, (3, 0, 2, 4, 1)).reshape(steps, 1, 4096)


def solution(mesh):
    placed = (
        P(None, ("req", "lend"), None),
        P(None, ("req", "lend"), None),
        P(None, ("req", "lend"), None),
        P(("req", "lend"), None, None),
        P(("req", "lend"), None, None),
        P(("req", "lend"), None, None),
        P(("req", "lend"), None, None),
        P(("req", "lend")),
        P(("req", "lend")),
        P(),
    )
    return jax.shard_map(
        on_device,
        mesh=mesh,
        in_specs=placed,
        out_specs=P(None, ("req", "lend"), None),
        check_vma=False,
    )
```

```python
import functools

import jax
import jax.numpy as jnp
from jax import lax
from jax.experimental import pallas as pl
from jax.experimental.pallas import tpu as pltpu
from jax.sharding import PartitionSpec as P

FLOOR = -1e30
SCORE_SCALE = 0.125
BF = jnp.bfloat16
F32 = jnp.float32
MESH = pl.DeviceIdType.MESH
GROUPS = 4
MSG = 80


def kernel(
    dims,
    q_hbm,
    nk_hbm,
    nv_hbm,
    k_hbm,
    v_hbm,
    ks_hbm,
    vs_hbm,
    req_hbm,
    fill_hbm,
    sink_hbm,
    out,
    kraw,
    vraw,
    ks,
    vs,
    kd,
    vd,
    q0,
    q1,
    num0,
    num1,
    st0,
    st1,
    stage,
    landed,
    q_raw,
    q_rows,
    qt,
    fresh_raw,
    fresh_f32,
    req_vec,
    fill_vec,
    req_s,
    sink_s,
    slot_sub,
    int_vec,
    ints,
    load_sem,
    small_sem,
    qsend,
    qrecv,
    psend,
    precv,
):
    n_req, n_lend, pages, chunk, unroll, dunroll = dims
    chunks = pages // chunk
    slots = n_lend + n_req
    req = lax.axis_index("req")
    lend = lax.axis_index("lend")
    qbuf = (q0, q1)
    num = (num0, num1)
    st = (st0, st1)

    def loads(c):
        sl = pl.ds(c * chunk, chunk)
        pairs = ((k_hbm, kraw), (v_hbm, vraw), (ks_hbm, ks), (vs_hbm, vs))
        return [
            pltpu.make_async_copy(src.at[sl], dst.at[sl], load_sem.at[i, c])
            for i, (src, dst) in enumerate(pairs)
        ]

    smalls = [
        pltpu.make_async_copy(src, dst, small_sem.at[i])
        for i, (src, dst) in enumerate(
            (
                (q_hbm, q_raw),
                (req_hbm, req_vec),
                (req_hbm, req_s),
                (fill_hbm, fill_vec),
                (sink_hbm, sink_s),
                (nk_hbm, fresh_raw.at[0]),
                (nv_hbm, fresh_raw.at[1]),
            )
        )
    ]
    for copy in smalls:
        copy.start()
    for c in range(chunks):
        for copy in loads(c):
            copy.start()

    ring_n = n_lend // 2
    ring = lend // 2
    core = lend % 2
    sibling = (req, 2 * ring + 1 - core)
    row_lend = lambda k: 2 * lax.rem(ring + k, ring_n) + core
    cross_lend = lambda k: 2 * lax.rem(ring + k, ring_n) + 1 - core
    from_lend = lambda k: 2 * lax.rem(ring + ring_n - k, ring_n) + core
    row_peer = lambda k: (req, row_lend(k))
    col_peer = lambda k: (lax.rem(req + k, n_req), lend)

    def loop(lo, hi, fn):
        def go(k, carry):
            fn(k)
            return carry

        lax.fori_loop(lo, hi, go, 0)

    barrier = pltpu.get_barrier_semaphore()

    def greet(peer):
        pl.semaphore_signal(barrier, inc=1, device_id=peer, device_id_type=MESH)

    greet(sibling)
    loop(1, ring_n, lambda k: greet(row_peer(k)))
    loop(1, n_req, lambda k: greet(col_peer(k)))

    smalls[0].wait()
    for j in range(32):
        h, g, ap = j // 16, (j // 4) % 4, j % 4
        tile = q_raw[:, j * 128 : j * 128 + 128].astype(F32) * SCORE_SCALE
        q_rows[pl.ds(h * 64 + g * 16 + ap, 4, stride=4), :] = tile
    turned = q_rows[...].T
    low_lanes = lax.broadcasted_iota(jnp.int32, (64, 128), 1) < 64
    even, odd = turned[0:64], turned[64:128]
    qt[0] = jnp.where(low_lanes, even, pltpu.roll(odd, 64, 1)).astype(BF)
    qt[1] = jnp.where(low_lanes, pltpu.roll(even, 64, 1), odd).astype(BF)
    for h in range(2):
        qbuf[h][lend] = qt[h]
    pl.semaphore_wait(barrier, ring_n + n_req - 1)

    def q_copy(src, h, at, slot, peer):
        return pltpu.make_async_remote_copy(
            src_ref=src,
            dst_ref=qbuf[h].at[slot],
            send_sem=qsend.at[h, at],
            recv_sem=qrecv.at[h, at],
            device_id=peer,
            device_id_type=MESH,
        )

    def q_row(h, k):
        return q_copy(qt.at[h], h, k, lend, row_peer(k))

    def q_own(h):
        return q_copy(qt.at[h], h, ring_n, lend, sibling)

    def q_pass(h, k):
        slot = from_lend(k)
        return q_copy(qbuf[h].at[slot], h, ring_n + k, slot, sibling)

    def q_col(h, k):
        return q_copy(qt.at[h], h, n_lend + k, n_lend + req, col_peer(k))

    for h in range(2):
        loop(1, ring_n, lambda k: q_row(h, k).start())
        loop(1, n_req, lambda k: q_col(h, k).start())
        q_own(h).start()

    def forward(h):
        def go(k):
            q_row(h, k).wait_recv()
            q_pass(h, k).start()

        loop(1, ring_n, go)

    for copy in smalls[1:]:
        copy.wait()

    def slot_of(request):
        owner_req = request // n_lend
        return jnp.where(owner_req == req, request % n_lend, n_lend + owner_req)

    def spread_slot(p):
        slot_sub[pl.ds(p, 1), :] = jnp.full((1, 128), slot_of(req_s[0, p]), jnp.int32)

    loop(0, pages, spread_slot)
    slot_lane = slot_of(req_vec[...])
    sub = slot_sub[...]
    page_sub = lax.broadcasted_iota(jnp.int32, (pages, pages), 0)
    page_lane = lax.broadcasted_iota(jnp.int32, (pages, pages), 1)
    same = (sub[:, 0:pages] == slot_lane) & (page_sub < page_lane)
    prev = jnp.max(jnp.where(same, page_sub, -1), axis=0, keepdims=True)
    hit = sub == lax.broadcasted_iota(jnp.int32, (pages, 128), 1)
    last = jnp.where(hit, lax.broadcasted_iota(jnp.int32, (pages, 128), 0), -1)
    last = jnp.max(last, axis=0, keepdims=True)
    int_vec[0:1, 0:pages] = slot_lane
    int_vec[1:2, 0:pages] = jnp.where(prev < 0, pages, prev)
    int_vec[2:3, 0:pages] = fill_vec[...]
    int_vec[3:4, :] = jnp.where(last < 0, pages, last)
    ints_copy = pltpu.make_async_copy(int_vec, ints, small_sem.at[7])
    ints_copy.start()

    fresh_f32[...] = jnp.zeros((2, 16, 512), F32)
    for i in range(2):
        fresh_f32[i, 0:4, :] = fresh_raw[i].astype(F32)
    lane = lax.broadcasted_iota(jnp.int32, (1, 128), 1)
    lane_head = (lane // 16) % 4 * 8 + (lane % 4) * 2 + lane // 64
    sink_rows = []
    for h in range(2):
        x = jnp.zeros((1, 128), F32)
        for i in range(32):
            x = jnp.where(lane_head == i, sink_s[0, h * 32 + i], x)
        sink_rows.append(x)

    blk = lax.broadcasted_iota(jnp.int32, (48, 512), 0) % 16
    chan = lax.broadcasted_iota(jnp.int32, (48, 512), 1) // 32
    spread = (blk == chan).astype(F32).astype(BF)

    def dequant(p):
        s = ks[p]
        hi = s.astype(BF)
        rest = s - hi.astype(F32)
        mid = rest.astype(BF)
        low = (rest - mid.astype(F32)).astype(BF)
        parts = jnp.concatenate([hi, mid, low], axis=0)
        wide = lax.dot_general(
            parts, spread, (((0,), (0,)), ((), ())), preferred_element_type=F32
        )
        kd[p] = (kraw[p].astype(F32) * wide).astype(BF)
        vt = vraw[p].T
        sv = jnp.broadcast_to(vs[p][:, None, :], (16, 32, 128)).reshape(512, 128)
        vd[p] = (vt.astype(F32) * sv).astype(BF)

    for c in range(chunks):
        for copy in loads(c):
            copy.wait()

        def some(i, carry):
            for j in range(dunroll):
                dequant(c * chunk + i * dunroll + j)
            return carry

        lax.fori_loop(0, chunk // dunroll, some, 0)
        if c == chunks - 2:
            forward(0)

    ints_copy.wait()
    lane_group = lax.broadcasted_iota(jnp.int32, (64, 128), 1) // 16 % 4
    token = lax.broadcasted_iota(jnp.int32, (128, 128), 0)

    def block_diagonal(q):
        zero = jnp.zeros_like(q)
        return jnp.concatenate(
            [jnp.where(lane_group == g, q, zero) for g in range(GROUPS)], axis=0
        )

    def fold(wide):
        x = wide[0:64]
        for g in range(1, GROUPS):
            x = jnp.where(lane_group == g, wide[64 * g : 64 * g + 64], x)
        return x

    def page(p, h):
        slot = ints[0, p]
        fill = ints[2, p]
        qb = block_diagonal(qbuf[h][slot])
        s = jnp.dot(kd[p, :, h * 256 : h * 256 + 256], qb, preferred_element_type=F32)
        s = jnp.where(token < fill, s, FLOOR)
        top = jnp.max(s, axis=0, keepdims=True)
        w = jnp.exp(s - top)
        total = jnp.sum(w, axis=0, keepdims=True)
        wide = jnp.dot(
            vd[p, h * 256 : h * 256 + 256, :], w.astype(BF), preferred_element_type=F32
        )
        return top, total, fold(wide)

    def update(p, h, top, total, x):
        prev = ints[1, p]
        fill = ints[2, p]
        prev_stat = st[h][prev]
        prev_top, prev_total = prev_stat[0:1], prev_stat[1:2]
        best = jnp.maximum(prev_top, top)
        fa = jnp.exp(prev_top - best)
        fb = jnp.where(fill > 0, jnp.exp(top - best), 0.0)
        st[h][p, 0:1, :] = best
        st[h][p, 1:2, :] = prev_total * fa + total * fb
        num[h][p] = num[h][prev] * fa + x * fb

    row16 = lax.broadcasted_iota(jnp.int32, (16, 128), 0)

    def pack(best, total, x):
        bh = best.astype(BF).astype(F32)
        bm = (best - bh).astype(BF).astype(F32)
        bl = best - bh - bm
        th = total.astype(BF).astype(F32)
        tm = total - th
        rows = jnp.zeros((16, 128), F32)
        for i, part in enumerate((bh, bm, bl, th, tm)):
            rows = jnp.where(row16 == i, part, rows)
        return jnp.concatenate([x.astype(BF), rows.astype(BF)], axis=0)

    def unpack(msg):
        x = msg[0:64].astype(F32)
        rows = msg[64:80].astype(F32)
        best = rows[0:1] + rows[1:2] + rows[2:3]
        total = rows[3:4] + rows[4:5]
        return best, total, x

    def partial_copy(h, k, peer):
        return pltpu.make_async_remote_copy(
            src_ref=stage.at[h, k],
            dst_ref=landed.at[h, k],
            send_sem=psend.at[h, k],
            recv_sem=precv.at[h, k],
            device_id=peer,
            device_id_type=MESH,
        )

    def p_row(h, k):
        return partial_copy(h, k, row_peer(k))

    def p_cross(h, k):
        return partial_copy(h, ring_n + k, sibling)

    def p_col(h, k):
        return partial_copy(h, n_lend + k, col_peer(k))

    def mine(h, slot):
        at = ints[3, slot]
        stat = st[h][at]
        return stat[0:1], stat[1:2], num[h][at]

    def merge(one, two):
        best = jnp.maximum(one[0], two[0])
        fa = jnp.exp(one[0] - best)
        fb = jnp.exp(two[0] - best)
        return best, one[1] * fa + two[1] * fb, one[2] * fa + two[2] * fb

    def send_cross(h):
        def go(k):
            stage[h, ring_n + k] = pack(*mine(h, cross_lend(k)))
            p_cross(h, k).start()

        loop(0, ring_n, go)

    def send_col(h):
        def go(k):
            stage[h, n_lend + k] = pack(*mine(h, n_lend + lax.rem(req + k, n_req)))
            p_col(h, k).start()

        loop(1, n_req, go)

    def send_row(h):
        def go(k):
            p_cross(h, k).wait_recv()
            both = merge(mine(h, row_lend(k)), unpack(landed[h, ring_n + k]))
            stage[h, k] = pack(*both)
            p_row(h, k).start()

        loop(1, ring_n, go)

    u16 = lax.broadcasted_iota(jnp.int32, (16, 128), 0)
    step16 = (lax.broadcasted_iota(jnp.int32, (16, 128), 1) // 4) % 4

    def fresh(h):
        qb = block_diagonal(qt[h])
        s = jnp.dot(
            fresh_f32[0, :, h * 256 : h * 256 + 256].astype(BF), qb, preferred_element_type=F32
        )
        s = jnp.where(u16 <= step16, s, FLOOR)
        top = jnp.max(s, axis=0, keepdims=True)
        w = jnp.exp(s - top)
        total = jnp.sum(w, axis=0, keepdims=True)
        wide = lax.dot_general(
            fresh_f32[1, :, h * 256 : h * 256 + 256].astype(BF),
            w.astype(BF),
            (((0,), (0,)), ((), ())),
            preferred_element_type=F32,
        )
        return top, total, fold(wide)

    def attend(h, lo, hi):
        def some_pages(i, carry):
            done = [page(i * unroll + j, h) for j in range(unroll)]
            for j in range(unroll):
                update(i * unroll + j, h, *done[j])
            return carry

        lax.fori_loop(lo, hi, some_pages, 0)

    rounds = pages // unroll
    for h in range(2):
        num[h][pages] = jnp.zeros((64, 128), F32)
        st[h][pages] = jnp.where(
            lax.broadcasted_iota(jnp.int32, (8, 128), 0) == 0, FLOOR, 0.0
        )
    for h in range(2):
        loop(0, ring_n, lambda k: q_copy(qt.at[h], h, ring_n + k, lend, sibling).wait_recv())
        loop(1, n_req, lambda k: q_col(h, k).wait_recv())
        attend(h, 0, rounds // 2)
        if h == 0:
            forward(1)
        else:
            send_row(0)
        attend(h, rounds // 2, rounds)
        send_cross(h)
        send_col(h)

    bases = []
    for h in range(2):
        new = fresh(h)
        sink = sink_rows[h]
        base = merge(new, mine(h, lend))
        top = jnp.maximum(base[0], sink)
        fa = jnp.exp(base[0] - top)
        bases.append((top, base[1] * fa + jnp.exp(sink - top), base[2] * fa))
    send_row(1)

    for h in range(2):
        p_cross(h, 0).wait_recv()
        loop(1, n_req, lambda k: p_col(h, k).wait_recv())
        loop(1, ring_n, lambda k: p_row(h, k).wait_recv())

        def absorb(k, carry):
            return merge(carry, unpack(landed[h, k]))

        carry = merge(bases[h], unpack(landed[h, ring_n]))
        carry = lax.fori_loop(n_lend + 1, slots, absorb, carry)
        carry = lax.fori_loop(1, ring_n, absorb, carry)
        out[h] = (carry[2] / carry[1]).astype(BF)

    for h in range(2):
        loop(1, ring_n, lambda k: q_row(h, k).wait_send())
        q_own(h).wait_send()
        loop(1, ring_n, lambda k: q_pass(h, k).wait_send())
        loop(1, n_req, lambda k: q_col(h, k).wait_send())
        loop(1, ring_n, lambda k: p_row(h, k).wait_send())
        loop(0, ring_n, lambda k: p_cross(h, k).wait_send())
        loop(1, n_req, lambda k: p_col(h, k).wait_send())


def on_device(
    queries,
    new_keys,
    new_values,
    key_pool,
    value_pool,
    key_scale,
    value_scale,
    page_request,
    page_fill,
    sinks,
):
    steps = queries.shape[0]
    pages = key_pool.shape[0]
    n_lend = lax.axis_size("lend")
    n_req = lax.axis_size("req")
    slots = n_lend + n_req
    chunk = 6 if pages % 6 == 0 else 4
    dims = (n_req, n_lend, pages, chunk, 24 if pages % 48 == 0 else 4, chunk)
    vmem = pl.BlockSpec(memory_space=pltpu.VMEM)
    hbm = pl.BlockSpec(memory_space=pltpu.MemorySpace.HBM)
    dma = pltpu.SemaphoreType.DMA
    half = pl.pallas_call(
        functools.partial(kernel, dims),
        out_shape=jax.ShapeDtypeStruct((2, 64, 128), BF),
        in_specs=[hbm] * 10,
        out_specs=vmem,
        scratch_shapes=[
            pltpu.VMEM((pages, 128, 512), BF),
            pltpu.VMEM((pages, 128, 512), BF),
            pltpu.VMEM((pages, 16, 128), F32),
            pltpu.VMEM((pages, 16, 128), F32),
            pltpu.VMEM((pages, 128, 512), BF),
            pltpu.VMEM((pages, 512, 128), BF),
            pltpu.VMEM((slots, 64, 128), BF),
            pltpu.VMEM((slots, 64, 128), BF),
            pltpu.VMEM((pages + 1, 64, 128), F32),
            pltpu.VMEM((pages + 1, 64, 128), F32),
            pltpu.VMEM((pages + 1, 8, 128), F32),
            pltpu.VMEM((pages + 1, 8, 128), F32),
            pltpu.VMEM((2, slots, MSG, 128), BF),
            pltpu.VMEM((2, slots, MSG, 128), BF),
            pltpu.VMEM((4, 4096), BF),
            pltpu.VMEM((128, 128), F32),
            pltpu.VMEM((2, 64, 128), BF),
            pltpu.VMEM((2, 4, 512), BF),
            pltpu.VMEM((2, 16, 512), F32),
            pltpu.VMEM((1, pages), jnp.int32),
            pltpu.VMEM((1, pages), jnp.int32),
            pltpu.SMEM((1, pages), jnp.int32),
            pltpu.SMEM((1, 64), F32),
            pltpu.VMEM((pages, 128), jnp.int32),
            pltpu.VMEM((8, 128), jnp.int32),
            pltpu.SMEM((8, 128), jnp.int32),
            dma((4, pages // chunk)),
            dma((8,)),
            dma((2, slots)),
            dma((2, slots)),
            dma((2, slots)),
            dma((2, slots)),
        ],
        compiler_params=pltpu.CompilerParams(
            collective_id=0, has_side_effects=True, vmem_limit_bytes=63 * 2**20
        ),
    )(
        queries.reshape(steps, 4096),
        new_keys.reshape(steps, 512),
        new_values.reshape(steps, 512),
        key_pool,
        value_pool,
        key_scale,
        value_scale,
        page_request.reshape(1, pages),
        page_fill.reshape(1, pages),
        sinks.reshape(1, 64),
    )
    out = half.reshape(2, 64, 2, GROUPS, steps, 4)
    return jnp.transpose(out, (4, 0, 3, 5, 2, 1)).reshape(steps, 1, 4096)


def solution(mesh):
    placed = (
        P(None, ("req", "lend"), None),
        P(None, ("req", "lend"), None),
        P(None, ("req", "lend"), None),
        P(("req", "lend"), None, None),
        P(("req", "lend"), None, None),
        P(("req", "lend"), None, None),
        P(("req", "lend"), None, None),
        P(("req", "lend")),
        P(("req", "lend")),
        P(),
    )
    return jax.shard_map(
        on_device,
        mesh=mesh,
        in_specs=placed,
        out_specs=P(None, ("req", "lend"), None),
        check_vma=False,
    )
```

```python
import functools

import jax
import jax.numpy as jnp
from jax import lax
from jax.experimental import pallas as pl
from jax.experimental.pallas import tpu as pltpu
from jax.sharding import PartitionSpec as P

FLOOR = -1e30
SCORE_SCALE = 0.125
BF = jnp.bfloat16
F32 = jnp.float32
MESH = pl.DeviceIdType.MESH
GROUPS = 4
MSG = 80


def kernel(
    dims,
    q_hbm,
    nk_hbm,
    nv_hbm,
    k_hbm,
    v_hbm,
    ks_hbm,
    vs_hbm,
    req_hbm,
    fill_hbm,
    sink_hbm,
    out,
    kraw,
    vraw,
    ks,
    vs,
    kd,
    vd,
    q0,
    q1,
    num0,
    num1,
    st0,
    st1,
    stage,
    landed,
    q_raw,
    q_rows,
    qt,
    fresh_raw,
    fresh_f32,
    req_vec,
    fill_vec,
    req_s,
    sink_s,
    slot_sub,
    int_vec,
    ints,
    load_sem,
    small_sem,
    qsend,
    qrecv,
    psend,
    precv,
):
    n_req, n_lend, pages, chunk, unroll, dunroll = dims
    chunks = pages // chunk
    slots = n_lend + n_req
    req = lax.axis_index("req")
    lend = lax.axis_index("lend")
    qbuf = (q0, q1)
    num = (num0, num1)
    st = (st0, st1)

    def loads(c):
        sl = pl.ds(c * chunk, chunk)
        pairs = ((k_hbm, kraw), (v_hbm, vraw), (ks_hbm, ks), (vs_hbm, vs))
        return [
            pltpu.make_async_copy(src.at[sl], dst.at[sl], load_sem.at[i, c])
            for i, (src, dst) in enumerate(pairs)
        ]

    smalls = [
        pltpu.make_async_copy(src, dst, small_sem.at[i])
        for i, (src, dst) in enumerate(
            (
                (q_hbm, q_raw),
                (req_hbm, req_vec),
                (req_hbm, req_s),
                (fill_hbm, fill_vec),
                (sink_hbm, sink_s),
                (nk_hbm, fresh_raw.at[0]),
                (nv_hbm, fresh_raw.at[1]),
            )
        )
    ]
    ring_n = n_lend // 2
    ring = lend // 2
    core = lend % 2
    sibling = (req, 2 * ring + 1 - core)
    row_lend = lambda k: 2 * lax.rem(ring + k, ring_n) + core
    cross_lend = lambda k: 2 * lax.rem(ring + k, ring_n) + 1 - core
    from_lend = lambda k: 2 * lax.rem(ring + ring_n - k, ring_n) + core
    row_peer = lambda k: (req, row_lend(k))
    xs = 4 if n_req % 4 == 0 else n_req
    ys = n_req // xs

    def col_req(k):
        y = lax.rem(req // xs + k // xs, ys)
        return y * xs + lax.rem(req % xs + k % xs, xs)

    col_peer = lambda k: (col_req(k), lend)
    cross_peer = lambda k: (req, cross_lend(k))
    hops = lambda k: min(k, ring_n - k)
    near_first = sorted(range(1, ring_n), key=hops)
    far = [k for k in near_first if hops(k) >= 3]
    far_q = (far, [])
    far_p = ([], far)

    def loop(lo, hi, fn):
        def go(k, carry):
            fn(k)
            return carry

        lax.fori_loop(lo, hi, go, 0)

    barrier = pltpu.get_barrier_semaphore()

    def greet(peer):
        pl.semaphore_signal(barrier, inc=1, device_id=peer, device_id_type=MESH)

    greet(sibling)
    loop(1, ring_n, lambda k: greet(row_peer(k)))
    loop(1, n_req, lambda k: greet(col_peer(k)))
    for k in far:
        greet(cross_peer(k))

    for copy in smalls:
        copy.start()
    for c in range(chunks):
        for copy in loads(c):
            copy.start()

    blk = lax.broadcasted_iota(jnp.int32, (48, 512), 0) % 16
    chan = lax.broadcasted_iota(jnp.int32, (48, 512), 1) // 32
    spread = (blk == chan).astype(F32).astype(BF)

    def dequant(p):
        s = ks[p]
        hi = s.astype(BF)
        rest = s - hi.astype(F32)
        mid = rest.astype(BF)
        low = (rest - mid.astype(F32)).astype(BF)
        parts = jnp.concatenate([hi, mid, low], axis=0)
        wide = lax.dot_general(
            parts, spread, (((0,), (0,)), ((), ())), preferred_element_type=F32
        )
        kd[p] = (kraw[p].astype(F32) * wide).astype(BF)
        vt = vraw[p].T
        sv = jnp.broadcast_to(vs[p][:, None, :], (16, 32, 128)).reshape(512, 128)
        vd[p] = (vt.astype(F32) * sv).astype(BF)

    def dequant_chunk(c):
        for copy in loads(c):
            copy.wait()

        def some(i, carry):
            for j in range(dunroll):
                dequant(c * chunk + i * dunroll + j)
            return carry

        lax.fori_loop(0, chunk // dunroll, some, 0)

    smalls[0].wait()
    for j in range(32):
        h, g, ap = j // 16, (j // 4) % 4, j % 4
        tile = q_raw[:, j * 128 : j * 128 + 128].astype(F32) * SCORE_SCALE
        q_rows[pl.ds(h * 64 + g * 16 + ap, 4, stride=4), :] = tile
    turned = q_rows[...].T
    low_lanes = lax.broadcasted_iota(jnp.int32, (64, 128), 1) < 64
    even, odd = turned[0:64], turned[64:128]
    qt[0] = jnp.where(low_lanes, even, pltpu.roll(odd, 64, 1)).astype(BF)
    qt[1] = jnp.where(low_lanes, pltpu.roll(even, 64, 1), odd).astype(BF)
    for h in range(2):
        qbuf[h][lend] = qt[h]
    early = min(3, chunks - 1)
    for c in range(early):
        dequant_chunk(c)
    pl.semaphore_wait(barrier, ring_n + n_req - 1 + len(far))

    def q_copy(src, h, at, slot, peer):
        return pltpu.make_async_remote_copy(
            src_ref=src,
            dst_ref=qbuf[h].at[slot],
            send_sem=qsend.at[h, at],
            recv_sem=qrecv.at[h, at],
            device_id=peer,
            device_id_type=MESH,
        )

    def q_row(h, k):
        return q_copy(qt.at[h], h, k, lend, row_peer(k))

    def q_own(h):
        return q_copy(qt.at[h], h, ring_n, lend, sibling)

    def q_cross(h, k):
        return q_copy(qt.at[h], h, ring_n + k, lend, cross_peer(k))

    def q_pass(h, k):
        slot = from_lend(k)
        return q_copy(qbuf[h].at[slot], h, ring_n + k, slot, sibling)

    def q_col(h, k):
        return q_copy(qt.at[h], h, n_lend + k, n_lend + req, col_peer(k))

    for h in range(2):
        for k in reversed(near_first):
            q_row(h, k).start()
            if k in far_q[h]:
                q_cross(h, k).start()
        loop(1, n_req, lambda k: q_col(h, n_req - k).start())
        q_own(h).start()

    def forward(h):
        for k in near_first:
            q_row(h, k).wait_recv()
            if k not in far_q[h]:
                q_pass(h, k).start()

    for copy in smalls[1:]:
        copy.wait()

    def slot_of(request):
        owner_req = request // n_lend
        return jnp.where(owner_req == req, request % n_lend, n_lend + owner_req)

    def spread_slot(p):
        slot_sub[pl.ds(p, 1), :] = jnp.full((1, 128), slot_of(req_s[0, p]), jnp.int32)

    loop(0, pages, spread_slot)
    slot_lane = slot_of(req_vec[...])
    sub = slot_sub[...]
    page_sub = lax.broadcasted_iota(jnp.int32, (pages, pages), 0)
    page_lane = lax.broadcasted_iota(jnp.int32, (pages, pages), 1)
    same = (sub[:, 0:pages] == slot_lane) & (page_sub < page_lane)
    prev = jnp.max(jnp.where(same, page_sub, -1), axis=0, keepdims=True)
    hit = sub == lax.broadcasted_iota(jnp.int32, (pages, 128), 1)
    last = jnp.where(hit, lax.broadcasted_iota(jnp.int32, (pages, 128), 0), -1)
    last = jnp.max(last, axis=0, keepdims=True)
    int_vec[0:1, 0:pages] = slot_lane
    int_vec[1:2, 0:pages] = jnp.where(prev < 0, pages, prev)
    int_vec[2:3, 0:pages] = fill_vec[...]
    int_vec[3:4, :] = jnp.where(last < 0, pages, last)
    ints_copy = pltpu.make_async_copy(int_vec, ints, small_sem.at[7])
    ints_copy.start()

    fresh_f32[...] = jnp.zeros((2, 16, 512), F32)
    for i in range(2):
        fresh_f32[i, 0:4, :] = fresh_raw[i].astype(F32)
    lane = lax.broadcasted_iota(jnp.int32, (1, 128), 1)
    lane_head = (lane // 16) % 4 * 8 + (lane % 4) * 2 + lane // 64
    sink_rows = []
    for h in range(2):
        x = jnp.zeros((1, 128), F32)
        for i in range(32):
            x = jnp.where(lane_head == i, sink_s[0, h * 32 + i], x)
        sink_rows.append(x)

    lane_group = lax.broadcasted_iota(jnp.int32, (64, 128), 1) // 16 % 4
    token = lax.broadcasted_iota(jnp.int32, (128, 128), 0)

    def block_diagonal(q):
        zero = jnp.zeros_like(q)
        return jnp.concatenate(
            [jnp.where(lane_group == g, q, zero) for g in range(GROUPS)], axis=0
        )

    def fold(wide):
        x = wide[0:64]
        for g in range(1, GROUPS):
            x = jnp.where(lane_group == g, wide[64 * g : 64 * g + 64], x)
        return x

    u16 = lax.broadcasted_iota(jnp.int32, (16, 128), 0)
    step16 = (lax.broadcasted_iota(jnp.int32, (16, 128), 1) // 4) % 4

    def fresh(h):
        qb = block_diagonal(qt[h])
        s = jnp.dot(
            fresh_f32[0, :, h * 256 : h * 256 + 256].astype(BF), qb, preferred_element_type=F32
        )
        s = jnp.where(u16 <= step16, s, FLOOR)
        top = jnp.max(s, axis=0, keepdims=True)
        w = jnp.exp(s - top)
        total = jnp.sum(w, axis=0, keepdims=True)
        wide = lax.dot_general(
            fresh_f32[1, :, h * 256 : h * 256 + 256].astype(BF),
            w.astype(BF),
            (((0,), (0,)), ((), ())),
            preferred_element_type=F32,
        )
        return top, total, fold(wide)

    news = [fresh(h) for h in range(2)]
    for c in range(early, chunks):
        dequant_chunk(c)
    forward(0)
    ints_copy.wait()
    def page(p, h):
        slot = ints[0, p]
        fill = ints[2, p]
        qb = block_diagonal(qbuf[h][slot])
        s = jnp.dot(kd[p, :, h * 256 : h * 256 + 256], qb, preferred_element_type=F32)
        s = jnp.where(token < fill, s, FLOOR)
        top = jnp.max(s, axis=0, keepdims=True)
        w = jnp.exp(s - top)
        total = jnp.sum(w, axis=0, keepdims=True)
        wide = jnp.dot(
            vd[p, h * 256 : h * 256 + 256, :], w.astype(BF), preferred_element_type=F32
        )
        return top, total, fold(wide)

    def update(p, h, top, total, x):
        prev = ints[1, p]
        fill = ints[2, p]
        prev_stat = st[h][prev]
        prev_top, prev_total = prev_stat[0:1], prev_stat[1:2]
        best = jnp.maximum(prev_top, top)
        fa = jnp.exp(prev_top - best)
        fb = jnp.where(fill > 0, jnp.exp(top - best), 0.0)
        st[h][p, 0:1, :] = best
        st[h][p, 1:2, :] = prev_total * fa + total * fb
        num[h][p] = num[h][prev] * fa + x * fb

    row16 = lax.broadcasted_iota(jnp.int32, (16, 128), 0)

    def pack(best, total, x):
        bh = best.astype(BF).astype(F32)
        bm = (best - bh).astype(BF).astype(F32)
        bl = best - bh - bm
        th = total.astype(BF).astype(F32)
        tm = total - th
        rows = jnp.zeros((16, 128), F32)
        for i, part in enumerate((bh, bm, bl, th, tm)):
            rows = jnp.where(row16 == i, part, rows)
        return jnp.concatenate([x.astype(BF), rows.astype(BF)], axis=0)

    def unpack(msg):
        x = msg[0:64].astype(F32)
        rows = msg[64:80].astype(F32)
        best = rows[0:1] + rows[1:2] + rows[2:3]
        total = rows[3:4] + rows[4:5]
        return best, total, x

    def partial_copy(h, k, peer):
        return pltpu.make_async_remote_copy(
            src_ref=stage.at[h, k],
            dst_ref=landed.at[h, k],
            send_sem=psend.at[h, k],
            recv_sem=precv.at[h, k],
            device_id=peer,
            device_id_type=MESH,
        )

    def p_row(h, k):
        return partial_copy(h, k, row_peer(k))

    def p_cross(h, k):
        return partial_copy(h, ring_n + k, sibling)

    def p_col(h, k):
        return partial_copy(h, n_lend + k, col_peer(k))

    def mine(h, slot):
        at = ints[3, slot]
        stat = st[h][at]
        return stat[0:1], stat[1:2], num[h][at]

    def merge(one, two):
        best = jnp.maximum(one[0], two[0])
        fa = jnp.exp(one[0] - best)
        fb = jnp.exp(two[0] - best)
        return best, one[1] * fa + two[1] * fb, one[2] * fa + two[2] * fb

    def p_far(h, k):
        return partial_copy(h, ring_n + k, cross_peer(k))

    def send_cross(h):
        for k in reversed([0] + near_first):
            stage[h, ring_n + k] = pack(*mine(h, cross_lend(k)))
            if k in far_p[h]:
                p_far(h, k).start()
                stage[h, k] = pack(*mine(h, row_lend(k)))
                p_row(h, k).start()
            else:
                p_cross(h, k).start()

    def send_col(h):
        def go(k):
            stage[h, n_lend + k] = pack(*mine(h, n_lend + col_req(k)))
            p_col(h, k).start()

        loop(1, n_req, go)

    def send_row(h):
        for k in reversed(near_first):
            if k not in far_p[h]:
                p_cross(h, k).wait_recv()
                both = merge(mine(h, row_lend(k)), unpack(landed[h, ring_n + k]))
                stage[h, k] = pack(*both)
                p_row(h, k).start()

    def attend(h, lo, hi):
        def some_pages(i, carry):
            done = [page(i * unroll + j, h) for j in range(unroll)]
            for j in range(unroll):
                update(i * unroll + j, h, *done[j])
            return carry

        lax.fori_loop(lo, hi, some_pages, 0)

    rounds = pages // unroll
    for h in range(2):
        num[h][pages] = jnp.zeros((64, 128), F32)
        st[h][pages] = jnp.where(
            lax.broadcasted_iota(jnp.int32, (8, 128), 0) == 0, FLOOR, 0.0
        )
    for h in range(2):
        loop(0, ring_n, lambda k: q_copy(qt.at[h], h, ring_n + k, lend, sibling).wait_recv())
        loop(1, n_req, lambda k: q_col(h, k).wait_recv())
        attend(h, 0, rounds // 2)
        if h == 0:
            forward(1)
        else:
            send_row(0)
        attend(h, rounds // 2, rounds)
        send_cross(h)
        send_col(h)

    send_row(1)

    halves = []
    for h in range(2):
        sink = sink_rows[h]
        base = merge(news[h], mine(h, lend))
        top = jnp.maximum(base[0], sink)
        fa = jnp.exp(base[0] - top)
        carry = (top, base[1] * fa + jnp.exp(sink - top), base[2] * fa)

        def absorb(at, carry):
            return merge(carry, unpack(landed[h, at]))

        p_cross(h, 0).wait_recv()
        carry = absorb(ring_n, carry)

        def absorb_col(k, carry):
            p_col(h, k).wait_recv()
            return absorb(n_lend + k, carry)

        carry = lax.fori_loop(1, n_req, absorb_col, carry)
        for k in near_first:
            p_row(h, k).wait_recv()
            carry = absorb(k, carry)
            if k in far_p[h]:
                p_far(h, k).wait_recv()
                carry = absorb(ring_n + k, carry)
        halves.append(carry[2] / carry[1])

    even = jnp.where(low_lanes, halves[0], pltpu.roll(halves[1], 64, 1))
    odd = jnp.where(low_lanes, pltpu.roll(halves[0], 64, 1), halves[1])
    q_rows[...] = jnp.concatenate([even, odd], axis=0).T
    for j in range(32):
        h, g, ap = j // 16, (j // 4) % 4, j % 4
        tile = q_rows[pl.ds(h * 64 + g * 16 + ap, 4, stride=4), :]
        out[:, j * 128 : j * 128 + 128] = tile.astype(BF)

    for h in range(2):
        q_own(h).wait_send()
        for k in near_first:
            q_row(h, k).wait_send()
            (q_cross if k in far_q[h] else q_pass)(h, k).wait_send()
            p_row(h, k).wait_send()
            (p_far if k in far_p[h] else p_cross)(h, k).wait_send()
        p_cross(h, 0).wait_send()
        loop(1, n_req, lambda k: q_col(h, k).wait_send())
        loop(1, n_req, lambda k: p_col(h, k).wait_send())


def on_device(
    queries,
    new_keys,
    new_values,
    key_pool,
    value_pool,
    key_scale,
    value_scale,
    page_request,
    page_fill,
    sinks,
):
    steps = queries.shape[0]
    pages = key_pool.shape[0]
    n_lend = lax.axis_size("lend")
    n_req = lax.axis_size("req")
    slots = n_lend + n_req
    chunk = 6 if pages % 6 == 0 else 4
    dims = (n_req, n_lend, pages, chunk, 24 if pages % 48 == 0 else 4, chunk)
    vmem = pl.BlockSpec(memory_space=pltpu.VMEM)
    hbm = pl.BlockSpec(memory_space=pltpu.MemorySpace.HBM)
    dma = pltpu.SemaphoreType.DMA
    out = pl.pallas_call(
        functools.partial(kernel, dims),
        out_shape=jax.ShapeDtypeStruct((4, 4096), BF),
        in_specs=[hbm] * 10,
        out_specs=vmem,
        scratch_shapes=[
            pltpu.VMEM((pages, 128, 512), BF),
            pltpu.VMEM((pages, 128, 512), BF),
            pltpu.VMEM((pages, 16, 128), F32),
            pltpu.VMEM((pages, 16, 128), F32),
            pltpu.VMEM((pages, 128, 512), BF),
            pltpu.VMEM((pages, 512, 128), BF),
            pltpu.VMEM((slots, 64, 128), BF),
            pltpu.VMEM((slots, 64, 128), BF),
            pltpu.VMEM((pages + 1, 64, 128), F32),
            pltpu.VMEM((pages + 1, 64, 128), F32),
            pltpu.VMEM((pages + 1, 8, 128), F32),
            pltpu.VMEM((pages + 1, 8, 128), F32),
            pltpu.VMEM((2, slots, MSG, 128), BF),
            pltpu.VMEM((2, slots, MSG, 128), BF),
            pltpu.VMEM((4, 4096), BF),
            pltpu.VMEM((128, 128), F32),
            pltpu.VMEM((2, 64, 128), BF),
            pltpu.VMEM((2, 4, 512), BF),
            pltpu.VMEM((2, 16, 512), F32),
            pltpu.VMEM((1, pages), jnp.int32),
            pltpu.VMEM((1, pages), jnp.int32),
            pltpu.SMEM((1, pages), jnp.int32),
            pltpu.SMEM((1, 64), F32),
            pltpu.VMEM((pages, 128), jnp.int32),
            pltpu.VMEM((8, 128), jnp.int32),
            pltpu.SMEM((8, 128), jnp.int32),
            dma((4, pages // chunk)),
            dma((8,)),
            dma((2, slots)),
            dma((2, slots)),
            dma((2, slots)),
            dma((2, slots)),
        ],
        compiler_params=pltpu.CompilerParams(
            collective_id=0, has_side_effects=True, vmem_limit_bytes=63 * 2**20
        ),
    )(
        queries.reshape(steps, 4096),
        new_keys.reshape(steps, 512),
        new_values.reshape(steps, 512),
        key_pool,
        value_pool,
        key_scale,
        value_scale,
        page_request.reshape(1, pages),
        page_fill.reshape(1, pages),
        sinks.reshape(1, 64),
    )
    return out.reshape(steps, 1, 4096)


def solution(mesh):
    placed = (
        P(None, ("req", "lend"), None),
        P(None, ("req", "lend"), None),
        P(None, ("req", "lend"), None),
        P(("req", "lend"), None, None),
        P(("req", "lend"), None, None),
        P(("req", "lend"), None, None),
        P(("req", "lend"), None, None),
        P(("req", "lend")),
        P(("req", "lend")),
        P(),
    )
    return jax.shard_map(
        on_device,
        mesh=mesh,
        in_specs=placed,
        out_specs=P(None, ("req", "lend"), None),
        check_vma=False,
    )
```

```python
import functools

import jax
import jax.numpy as jnp
from jax import lax
from jax.experimental import pallas as pl
from jax.experimental.pallas import tpu as pltpu
from jax.sharding import PartitionSpec as P

FLOOR = -1e30
SCORE_SCALE = 0.125
BF = jnp.bfloat16
F32 = jnp.float32
MESH = pl.DeviceIdType.MESH
GROUPS = 4
MSG = 80


def kernel(
    dims,
    q_hbm,
    nk_hbm,
    nv_hbm,
    k_hbm,
    v_hbm,
    ks_hbm,
    vs_hbm,
    req_hbm,
    fill_hbm,
    sink_hbm,
    out,
    kraw,
    vraw,
    ks,
    vs,
    kd,
    vd,
    q0,
    q1,
    num0,
    num1,
    st0,
    st1,
    stage,
    landed,
    q_raw,
    q_rows,
    qt,
    fresh_raw,
    fresh_f32,
    req_vec,
    fill_vec,
    req_s,
    sink_s,
    slot_sub,
    int_vec,
    ints,
    load_sem,
    small_sem,
    qsend,
    qrecv,
    psend,
    precv,
):
    n_req, n_lend, pages, chunk, unroll, dunroll = dims
    chunks = pages // chunk
    slots = n_lend + n_req
    req = lax.axis_index("req")
    lend = lax.axis_index("lend")
    qbuf = (q0, q1)
    num = (num0, num1)
    st = (st0, st1)

    def loads(c):
        sl = pl.ds(c * chunk, chunk)
        pairs = ((k_hbm, kraw), (v_hbm, vraw), (ks_hbm, ks), (vs_hbm, vs))
        return [
            pltpu.make_async_copy(src.at[sl], dst.at[sl], load_sem.at[i, c])
            for i, (src, dst) in enumerate(pairs)
        ]

    smalls = [
        pltpu.make_async_copy(src, dst, small_sem.at[i])
        for i, (src, dst) in enumerate(
            (
                (q_hbm, q_raw),
                (req_hbm, req_vec),
                (req_hbm, req_s),
                (fill_hbm, fill_vec),
                (sink_hbm, sink_s),
                (nk_hbm, fresh_raw.at[0]),
                (nv_hbm, fresh_raw.at[1]),
            )
        )
    ]
    ring_n = n_lend // 2
    ring = lend // 2
    core = lend % 2
    sibling = (req, 2 * ring + 1 - core)
    row_lend = lambda k: 2 * lax.rem(ring + k, ring_n) + core
    cross_lend = lambda k: 2 * lax.rem(ring + k, ring_n) + 1 - core
    from_lend = lambda k: 2 * lax.rem(ring + ring_n - k, ring_n) + core
    row_peer = lambda k: (req, row_lend(k))
    xs = 4 if n_req % 4 == 0 else n_req
    ys = n_req // xs

    def col_req(k):
        y = lax.rem(req // xs + k // xs, ys)
        return y * xs + lax.rem(req % xs + k % xs, xs)

    col_peer = lambda k: (col_req(k), lend)
    hops = lambda k: min(k, ring_n - k)
    near_first = sorted(range(1, ring_n), key=hops)

    def loop(lo, hi, fn):
        def go(k, carry):
            fn(k)
            return carry

        lax.fori_loop(lo, hi, go, 0)

    barrier = pltpu.get_barrier_semaphore()

    def greet(peer):
        pl.semaphore_signal(barrier, inc=1, device_id=peer, device_id_type=MESH)

    greet(sibling)
    loop(1, ring_n, lambda k: greet(row_peer(k)))
    loop(1, n_req, lambda k: greet(col_peer(k)))

    for copy in smalls:
        copy.start()
    for c in range(chunks):
        for copy in loads(c):
            copy.start()

    blk = lax.broadcasted_iota(jnp.int32, (48, 512), 0) % 16
    chan = lax.broadcasted_iota(jnp.int32, (48, 512), 1) // 32
    spread = (blk == chan).astype(F32).astype(BF)

    def dequant(p):
        s = ks[p]
        hi = s.astype(BF)
        rest = s - hi.astype(F32)
        mid = rest.astype(BF)
        low = (rest - mid.astype(F32)).astype(BF)
        parts = jnp.concatenate([hi, mid, low], axis=0)
        wide = lax.dot_general(
            parts, spread, (((0,), (0,)), ((), ())), preferred_element_type=F32
        )
        kd[p] = (kraw[p].astype(F32) * wide).astype(BF)
        vt = vraw[p].T
        sv = jnp.broadcast_to(vs[p][:, None, :], (16, 32, 128)).reshape(512, 128)
        vd[p] = (vt.astype(F32) * sv).astype(BF)

    def dequant_chunk(c):
        for copy in loads(c):
            copy.wait()

        def some(i, carry):
            for j in range(dunroll):
                dequant(c * chunk + i * dunroll + j)
            return carry

        lax.fori_loop(0, chunk // dunroll, some, 0)

    smalls[0].wait()
    for j in range(32):
        h, g, ap = j // 16, (j // 4) % 4, j % 4
        tile = q_raw[:, j * 128 : j * 128 + 128].astype(F32) * SCORE_SCALE
        q_rows[pl.ds(h * 64 + g * 16 + ap, 4, stride=4), :] = tile
    turned = q_rows[...].T
    low_lanes = lax.broadcasted_iota(jnp.int32, (64, 128), 1) < 64
    even, odd = turned[0:64], turned[64:128]
    qt[0] = jnp.where(low_lanes, even, pltpu.roll(odd, 64, 1)).astype(BF)
    qt[1] = jnp.where(low_lanes, pltpu.roll(even, 64, 1), odd).astype(BF)
    for h in range(2):
        qbuf[h][lend] = qt[h]
    pl.semaphore_wait(barrier, ring_n + n_req - 1)

    def q_copy(src, h, at, slot, peer):
        return pltpu.make_async_remote_copy(
            src_ref=src,
            dst_ref=qbuf[h].at[slot],
            send_sem=qsend.at[h, at],
            recv_sem=qrecv.at[h, at],
            device_id=peer,
            device_id_type=MESH,
        )

    def q_row(h, k):
        return q_copy(qt.at[h], h, k, lend, row_peer(k))

    def q_own(h):
        return q_copy(qt.at[h], h, ring_n, lend, sibling)

    def q_pass(h, k):
        slot = from_lend(k)
        return q_copy(qbuf[h].at[slot], h, ring_n + k, slot, sibling)

    def q_col(h, k):
        return q_copy(qt.at[h], h, n_lend + k, n_lend + req, col_peer(k))

    for h in range(2):
        for k in reversed(near_first):
            q_row(h, k).start()
        loop(1, n_req, lambda k: q_col(h, n_req - k).start())
        q_own(h).start()

    def forward(h):
        for k in near_first:
            q_row(h, k).wait_recv()
            q_pass(h, k).start()

    for copy in smalls[1:]:
        copy.wait()

    def slot_of(request):
        owner_req = request // n_lend
        return jnp.where(owner_req == req, request % n_lend, n_lend + owner_req)

    def spread_slot(p):
        slot_sub[pl.ds(p, 1), :] = jnp.full((1, 128), slot_of(req_s[0, p]), jnp.int32)

    loop(0, pages, spread_slot)
    slot_lane = slot_of(req_vec[...])
    sub = slot_sub[...]
    page_sub = lax.broadcasted_iota(jnp.int32, (pages, pages), 0)
    page_lane = lax.broadcasted_iota(jnp.int32, (pages, pages), 1)
    same = (sub[:, 0:pages] == slot_lane) & (page_sub < page_lane)
    prev = jnp.max(jnp.where(same, page_sub, -1), axis=0, keepdims=True)
    hit = sub == lax.broadcasted_iota(jnp.int32, (pages, 128), 1)
    last = jnp.where(hit, lax.broadcasted_iota(jnp.int32, (pages, 128), 0), -1)
    last = jnp.max(last, axis=0, keepdims=True)
    int_vec[0:1, 0:pages] = slot_lane
    int_vec[1:2, 0:pages] = jnp.where(prev < 0, pages, prev)
    int_vec[2:3, 0:pages] = fill_vec[...]
    int_vec[3:4, :] = jnp.where(last < 0, pages, last)
    ints_copy = pltpu.make_async_copy(int_vec, ints, small_sem.at[7])
    ints_copy.start()

    fresh_f32[...] = jnp.zeros((2, 16, 512), F32)
    for i in range(2):
        fresh_f32[i, 0:4, :] = fresh_raw[i].astype(F32)
    lane = lax.broadcasted_iota(jnp.int32, (1, 128), 1)
    lane_head = (lane // 16) % 4 * 8 + (lane % 4) * 2 + lane // 64
    sink_rows = []
    for h in range(2):
        x = jnp.zeros((1, 128), F32)
        for i in range(32):
            x = jnp.where(lane_head == i, sink_s[0, h * 32 + i], x)
        sink_rows.append(x)

    lane_group = lax.broadcasted_iota(jnp.int32, (64, 128), 1) // 16 % 4
    token = lax.broadcasted_iota(jnp.int32, (128, 128), 0)

    def block_diagonal(q):
        zero = jnp.zeros_like(q)
        return jnp.concatenate(
            [jnp.where(lane_group == g, q, zero) for g in range(GROUPS)], axis=0
        )

    def fold(wide):
        x = wide[0:64]
        for g in range(1, GROUPS):
            x = jnp.where(lane_group == g, wide[64 * g : 64 * g + 64], x)
        return x

    u16 = lax.broadcasted_iota(jnp.int32, (16, 128), 0)
    step16 = (lax.broadcasted_iota(jnp.int32, (16, 128), 1) // 4) % 4

    def fresh(h):
        qb = block_diagonal(qt[h])
        s = jnp.dot(
            fresh_f32[0, :, h * 256 : h * 256 + 256].astype(BF), qb, preferred_element_type=F32
        )
        s = jnp.where(u16 <= step16, s, FLOOR)
        top = jnp.max(s, axis=0, keepdims=True)
        w = jnp.exp(s - top)
        total = jnp.sum(w, axis=0, keepdims=True)
        wide = lax.dot_general(
            fresh_f32[1, :, h * 256 : h * 256 + 256].astype(BF),
            w.astype(BF),
            (((0,), (0,)), ((), ())),
            preferred_element_type=F32,
        )
        return top, total, fold(wide)

    news = [fresh(h) for h in range(2)]
    for c in range(chunks):
        dequant_chunk(c)
    forward(0)
    ints_copy.wait()
    def page(p, h):
        slot = ints[0, p]
        fill = ints[2, p]
        qb = block_diagonal(qbuf[h][slot])
        s = jnp.dot(kd[p, :, h * 256 : h * 256 + 256], qb, preferred_element_type=F32)
        s = jnp.where(token < fill, s, FLOOR)
        top = jnp.max(s, axis=0, keepdims=True)
        w = jnp.exp(s - top)
        total = jnp.sum(w, axis=0, keepdims=True)
        wide = jnp.dot(
            vd[p, h * 256 : h * 256 + 256, :], w.astype(BF), preferred_element_type=F32
        )
        return top, total, fold(wide)

    def update(p, h, top, total, x):
        prev = ints[1, p]
        fill = ints[2, p]
        prev_stat = st[h][prev]
        prev_top, prev_total = prev_stat[0:1], prev_stat[1:2]
        best = jnp.maximum(prev_top, top)
        fa = jnp.exp(prev_top - best)
        fb = jnp.where(fill > 0, jnp.exp(top - best), 0.0)
        st[h][p, 0:1, :] = best
        st[h][p, 1:2, :] = prev_total * fa + total * fb
        num[h][p] = num[h][prev] * fa + x * fb

    row16 = lax.broadcasted_iota(jnp.int32, (16, 128), 0)

    def pack(best, total, x):
        bh = best.astype(BF).astype(F32)
        bm = (best - bh).astype(BF).astype(F32)
        bl = best - bh - bm
        th = total.astype(BF).astype(F32)
        tm = total - th
        rows = jnp.zeros((16, 128), F32)
        for i, part in enumerate((bh, bm, bl, th, tm)):
            rows = jnp.where(row16 == i, part, rows)
        return jnp.concatenate([x.astype(BF), rows.astype(BF)], axis=0)

    def unpack(msg):
        x = msg[0:64].astype(F32)
        rows = msg[64:80].astype(F32)
        best = rows[0:1] + rows[1:2] + rows[2:3]
        total = rows[3:4] + rows[4:5]
        return best, total, x

    def partial_copy(h, k, peer):
        return pltpu.make_async_remote_copy(
            src_ref=stage.at[h, k],
            dst_ref=landed.at[h, k],
            send_sem=psend.at[h, k],
            recv_sem=precv.at[h, k],
            device_id=peer,
            device_id_type=MESH,
        )

    def p_row(h, k):
        return partial_copy(h, k, row_peer(k))

    def p_cross(h, k):
        return partial_copy(h, ring_n + k, sibling)

    def p_col(h, k):
        return partial_copy(h, n_lend + k, col_peer(k))

    def mine(h, slot):
        at = ints[3, slot]
        stat = st[h][at]
        return stat[0:1], stat[1:2], num[h][at]

    def merge(one, two):
        best = jnp.maximum(one[0], two[0])
        fa = jnp.exp(one[0] - best)
        fb = jnp.exp(two[0] - best)
        return best, one[1] * fa + two[1] * fb, one[2] * fa + two[2] * fb

    def send_cross(h):
        order = list(reversed([0] + near_first))
        for at in range(0, ring_n, 4):
            some = order[at : at + 4]
            packed = [pack(*mine(h, cross_lend(k))) for k in some]
            for k, msg in zip(some, packed):
                stage[h, ring_n + k] = msg
            for k in some:
                p_cross(h, k).start()

    col_group = 5 if (n_req - 1) % 5 == 0 else 1

    def send_col(h):
        def go(i):
            some = [1 + i * col_group + j for j in range(col_group)]
            packed = [pack(*mine(h, n_lend + col_req(k))) for k in some]
            for k, msg in zip(some, packed):
                stage[h, n_lend + k] = msg
            for k in some:
                p_col(h, k).start()

        loop(0, (n_req - 1) // col_group, go)

    def send_row(h):
        order = list(reversed(near_first))
        for some in (order[:3], order[3:]):
            for k in some:
                p_cross(h, k).wait_recv()
            packed = [
                pack(*merge(mine(h, row_lend(k)), unpack(landed[h, ring_n + k])))
                for k in some
            ]
            for k, msg in zip(some, packed):
                stage[h, k] = msg
            for k in some:
                p_row(h, k).start()

    def attend(h, lo, hi):
        def some_pages(i, carry):
            done = [page(i * unroll + j, h) for j in range(unroll)]
            for j in range(unroll):
                update(i * unroll + j, h, *done[j])
            return carry

        lax.fori_loop(lo, hi, some_pages, 0)

    rounds = pages // unroll
    for h in range(2):
        num[h][pages] = jnp.zeros((64, 128), F32)
        st[h][pages] = jnp.where(
            lax.broadcasted_iota(jnp.int32, (8, 128), 0) == 0, FLOOR, 0.0
        )
    for h in range(2):
        loop(0, ring_n, lambda k: q_copy(qt.at[h], h, ring_n + k, lend, sibling).wait_recv())
        loop(1, n_req, lambda k: q_col(h, k).wait_recv())
        attend(h, 0, rounds // 2)
        if h == 0:
            forward(1)
        else:
            send_row(0)
        attend(h, rounds // 2, rounds)
        send_cross(h)
        send_col(h)

    send_row(1)

    halves = []
    for h in range(2):
        sink = sink_rows[h]
        base = merge(news[h], mine(h, lend))
        top = jnp.maximum(base[0], sink)
        fa = jnp.exp(base[0] - top)
        carry = (top, base[1] * fa + jnp.exp(sink - top), base[2] * fa)

        def absorb(at, carry):
            return merge(carry, unpack(landed[h, at]))

        p_cross(h, 0).wait_recv()
        carry = absorb(ring_n, carry)

        def absorb_col(k, carry):
            p_col(h, k).wait_recv()
            return absorb(n_lend + k, carry)

        carry = lax.fori_loop(1, n_req, absorb_col, carry)
        q_own(h).wait_send()
        p_cross(h, 0).wait_send()
        loop(1, n_req, lambda k: q_col(h, k).wait_send())
        loop(1, n_req, lambda k: p_col(h, k).wait_send())
        for k in near_first:
            q_row(h, k).wait_send()
            q_pass(h, k).wait_send()
            p_cross(h, k).wait_send()
            p_row(h, k).wait_send()
        for k in near_first:
            p_row(h, k).wait_recv()
            carry = absorb(k, carry)
        halves.append(carry[2] / carry[1])

    even = jnp.where(low_lanes, halves[0], pltpu.roll(halves[1], 64, 1))
    odd = jnp.where(low_lanes, pltpu.roll(halves[0], 64, 1), halves[1])
    q_rows[...] = jnp.concatenate([even, odd], axis=0).T
    for j in range(32):
        h, g, ap = j // 16, (j // 4) % 4, j % 4
        tile = q_rows[pl.ds(h * 64 + g * 16 + ap, 4, stride=4), :]
        out[:, j * 128 : j * 128 + 128] = tile.astype(BF)


def on_device(
    queries,
    new_keys,
    new_values,
    key_pool,
    value_pool,
    key_scale,
    value_scale,
    page_request,
    page_fill,
    sinks,
):
    steps = queries.shape[0]
    pages = key_pool.shape[0]
    n_lend = lax.axis_size("lend")
    n_req = lax.axis_size("req")
    slots = n_lend + n_req
    chunk = 6 if pages % 6 == 0 else 4
    dims = (n_req, n_lend, pages, chunk, 24 if pages % 48 == 0 else 4, chunk)
    vmem = pl.BlockSpec(memory_space=pltpu.VMEM)
    hbm = pl.BlockSpec(memory_space=pltpu.MemorySpace.HBM)
    dma = pltpu.SemaphoreType.DMA
    out = pl.pallas_call(
        functools.partial(kernel, dims),
        out_shape=jax.ShapeDtypeStruct((4, 4096), BF),
        in_specs=[hbm] * 10,
        out_specs=vmem,
        scratch_shapes=[
            pltpu.VMEM((pages, 128, 512), BF),
            pltpu.VMEM((pages, 128, 512), BF),
            pltpu.VMEM((pages, 16, 128), F32),
            pltpu.VMEM((pages, 16, 128), F32),
            pltpu.VMEM((pages, 128, 512), BF),
            pltpu.VMEM((pages, 512, 128), BF),
            pltpu.VMEM((slots, 64, 128), BF),
            pltpu.VMEM((slots, 64, 128), BF),
            pltpu.VMEM((pages + 1, 64, 128), F32),
            pltpu.VMEM((pages + 1, 64, 128), F32),
            pltpu.VMEM((pages + 1, 8, 128), F32),
            pltpu.VMEM((pages + 1, 8, 128), F32),
            pltpu.VMEM((2, slots, MSG, 128), BF),
            pltpu.VMEM((2, slots, MSG, 128), BF),
            pltpu.VMEM((4, 4096), BF),
            pltpu.VMEM((128, 128), F32),
            pltpu.VMEM((2, 64, 128), BF),
            pltpu.VMEM((2, 4, 512), BF),
            pltpu.VMEM((2, 16, 512), F32),
            pltpu.VMEM((1, pages), jnp.int32),
            pltpu.VMEM((1, pages), jnp.int32),
            pltpu.SMEM((1, pages), jnp.int32),
            pltpu.SMEM((1, 64), F32),
            pltpu.VMEM((pages, 128), jnp.int32),
            pltpu.VMEM((8, 128), jnp.int32),
            pltpu.SMEM((8, 128), jnp.int32),
            dma((4, pages // chunk)),
            dma((8,)),
            dma((2, slots)),
            dma((2, slots)),
            dma((2, slots)),
            dma((2, slots)),
        ],
        compiler_params=pltpu.CompilerParams(
            collective_id=0, has_side_effects=True, vmem_limit_bytes=63 * 2**20
        ),
    )(
        queries.reshape(steps, 4096),
        new_keys.reshape(steps, 512),
        new_values.reshape(steps, 512),
        key_pool,
        value_pool,
        key_scale,
        value_scale,
        page_request.reshape(1, pages),
        page_fill.reshape(1, pages),
        sinks.reshape(1, 64),
    )
    return out.reshape(steps, 1, 4096)


def solution(mesh):
    placed = (
        P(None, ("req", "lend"), None),
        P(None, ("req", "lend"), None),
        P(None, ("req", "lend"), None),
        P(("req", "lend"), None, None),
        P(("req", "lend"), None, None),
        P(("req", "lend"), None, None),
        P(("req", "lend"), None, None),
        P(("req", "lend")),
        P(("req", "lend")),
        P(),
    )
    return jax.shard_map(
        on_device,
        mesh=mesh,
        in_specs=placed,
        out_specs=P(None, ("req", "lend"), None),
        check_vma=False,
    )
```
